32 devices in a mesh: grp: 2 (over y), inst: 4 (over x, core), tp: 4 (over z).
Axes of the slice: x: 2, y: 2, z: 4, core: 2. Of those that a mesh axis runs over, the one named last changes fastest.
Arguments:
- kv_pool: bfloat16 [8, 512, 8, 16, 256], P(('grp', 'inst'), None, 'tp'), parts along dimension 0, may hold values from -6 to 6, as said below
- block_table: int32 [8, 16, 32], P(('grp', 'inst')), parts along dimension 0, may hold values from 0 to 511, as said below
- lengths: int32 [8, 16], P('grp'), parts along dimension 0, may hold values from 0 to 512, as said below
- pairs: int32 [4, 2], P('grp'), parts along dimension 0, may hold values from 0 to 3, as said below
- moved: int32 [4, 2], P('grp'), parts along dimension 0, may hold values from 0 to 15, as said below
- queries: bfloat16 [2, 128, 8192], P(None, ('grp', 'inst'), 'tp'), parts along dimension 1, may hold values from -200 to 200
- fresh_kv: bfloat16 [2, 128, 2048], P(None, ('grp', 'inst'), 'tp'), parts along dimension 1, may hold values from -6 to 6, as said below
- out_weight: bfloat16 [8192, 8192], P('tp'), may hold values from -0.0625 to 0.0625
Outputs:
- layer_out: bfloat16 [2, 128, 8192], P(None, ('grp', 'inst'), 'tp'), parts along dimension 1
The draws below stay inside these ranges and needn't reach their ends.
There are 2 independent parts, one for each index of `grp`. The reference program is written for one: setup_inputs(seed, part) draws one part's arguments, and reference() takes and returns one part's arrays. A program takes and returns all parts, laid end to end along the dimension named above; an argument that names none is the same for every part. Nothing has to cross between parts.
Inputs may be any that keep to these rules, and one draw needn't show every extreme that they name: `pairs`: each instance stands in at most one pair. `moved`: the slots of one pair are distinct. `lengths`: slots moved[p, :] hold 0 at instance pairs[p, 1]; every other slot holds 1 or more; moved[p, 0] holds 512 at instance pairs[p, 0]. `block_table`: each instance's table names each of its 512 blocks once. `kv_pool`: slots j and j' of the third dimension are equal where j = j'. `fresh_kv`: slots j and j' are equal where j = j'.
All inputs are finite; a program needn't handle non-finite values.
Results may differ from the reference program's by a relative error of at most 0.0058.
Values may be sent and summed in bfloat16 or wider, within the bound.
A program may use at most 128 MiB of HBM per device.

```python
import math
import jax
import jax.numpy as jnp
from jax import lax

D = 8192
HEADS = 64
KVH = 8
HD = 128
REQ = 16
CTX = 512
BLK = 16
MIG = 2
STEPS = 2
NBLK = 32
POOL = 512
KVS = 8
REP = 1
GQA = 8
ROWS = 64
PAIRS = 2
N_INST = 4


def shared_routes(key):
    order = jax.random.permutation(jax.random.fold_in(key, 101), N_INST).astype(jnp.int32)
    pair_list = jnp.stack([order[:PAIRS], order[PAIRS:2 * PAIRS]], axis=1)
    pair_keys = jax.random.split(jax.random.fold_in(key, 102), PAIRS)
    slots = jax.vmap(lambda k: jax.random.permutation(k, REQ - 1)[:MIG])(pair_keys).astype(jnp.int32)
    slots = slots.at[0, MIG - 1].set(REQ - 1)
    slots = slots.at[0, 0].set(0)
    return (pair_list, slots.astype(jnp.int32))


def shared_keys(key):
    return jax.random.normal(jax.random.fold_in(key, 201), (STEPS, ROWS, KVH, HD), jnp.float32)


def draw_pairs(key, part):
    pair_list, slots = shared_routes(key)
    return pair_list


def draw_moved(key, part):
    pair_list, slots = shared_routes(key)
    return slots


def draw_lengths(key, part):
    pair_list, slots = shared_routes(key)
    key = jax.random.fold_in(key, 3)
    loaded = jnp.any(pair_list[:, 0][:, None] == jnp.arange(N_INST)[None, :], axis=0)
    long_side = jax.random.randint(jax.random.fold_in(key, 1), (N_INST, REQ), CTX // 2, CTX + 1)
    short_side = jax.random.randint(jax.random.fold_in(key, 2), (N_INST, REQ), 1, CTX // 4 + 1)
    lens = jnp.where(loaded[:, None], long_side, short_side).astype(jnp.int32)
    lens = lens.at[pair_list[:, 0], slots[:, 0]].set(CTX)
    lens = lens.at[pair_list[:, 1][:, None], slots].set(0)
    return lens.astype(jnp.int32)


def draw_block_table(key, part):
    key = jax.random.fold_in(key, 4)
    inst_keys = jax.random.split(key, N_INST)
    tables = jax.vmap(lambda k: jax.random.permutation(k, POOL))(inst_keys)
    return tables.reshape(N_INST, REQ, NBLK).astype(jnp.int32)


def draw_kv_pool(key, part):
    key = jax.random.fold_in(key, 7)
    heads = jnp.clip(jax.random.normal(key, (N_INST, POOL, KVH, BLK, 2 * HD), jnp.float32), -6.0, 6.0)
    return jnp.repeat(heads, REP, axis=2).astype(jnp.bfloat16)


def draw_fresh_kv(key, part):
    base = shared_keys(key)
    key = jax.random.fold_in(key, 5)
    keys_part = jnp.clip(base, -6.0, 6.0)
    values = jnp.clip(jax.random.normal(key, (STEPS, ROWS, KVH, HD), jnp.float32), -6.0, 6.0)
    joined = jnp.concatenate([keys_part, values], axis=-1)
    joined = jnp.repeat(joined, REP, axis=2)
    return joined.reshape(STEPS, ROWS, KVS * 2 * HD).astype(jnp.bfloat16)


def draw_queries(key, part):
    key = jax.random.fold_in(key, 6)
    values = jnp.clip(jax.random.normal(key, (STEPS, ROWS, HEADS, HD), jnp.float32), -6.0, 6.0)
    return values.reshape(STEPS, ROWS, HEADS * HD).astype(jnp.bfloat16)


def block_levels(key, dims, cuts, low, high):
    loudness, own = 1.0, jax.random.fold_in(key, 6)
    for dim, parts in cuts:
        heights = jnp.exp(jax.random.uniform(jax.random.fold_in(own, dim), (parts,), jnp.float32, low / len(cuts), high / len(cuts)))
        loudness = loudness * jnp.repeat(heights, dims[dim] // parts).reshape([-1 if axis == dim else 1 for axis in range(len(dims))])
    return loudness


def noise(rng, extent, spread, bound, pieces=(), kind=jnp.bfloat16):
    result = spread * jax.random.normal(rng, extent, jnp.float32)
    if pieces:
        result = result * block_levels(rng, extent, pieces, -0.22, 0.18)
    return jnp.clip(result, -bound, bound).astype(kind)


def setup_inputs(seed: int = 0, part: int = 0) -> dict:
    key_list = jax.random.split(jax.random.key(seed), 9)
    part_keys = jax.random.split(jax.random.fold_in(key_list[8], part), 9)
    kv_pool = draw_kv_pool(jax.random.fold_in(jax.random.fold_in(key_list[8], part), 71), part)
    block_table = draw_block_table(jax.random.fold_in(jax.random.fold_in(key_list[8], part), 71), part)
    lengths = draw_lengths(jax.random.fold_in(jax.random.fold_in(key_list[8], part), 71), part)
    pairs = draw_pairs(jax.random.fold_in(jax.random.fold_in(key_list[8], part), 71), part)
    moved = draw_moved(jax.random.fold_in(jax.random.fold_in(key_list[8], part), 71), part)
    queries = draw_queries(jax.random.fold_in(jax.random.fold_in(key_list[8], part), 71), part)
    fresh_kv = draw_fresh_kv(jax.random.fold_in(jax.random.fold_in(key_list[8], part), 71), part)
    out_weight = noise(key_list[7], (HEADS * HD, D), (HEADS * HD) ** -0.5, 0.0625, ((0, 4),))
    return {"kv_pool": kv_pool, "block_table": block_table, "lengths": lengths, "pairs": pairs, "moved": moved, "queries": queries, "fresh_kv": fresh_kv, "out_weight": out_weight}


def reference(kv_pool, block_table, lengths, pairs, moved, queries, fresh_kv, out_weight):
    inst_ids = jnp.arange(N_INST, dtype=jnp.int32)
    slot_ids = jnp.arange(REQ, dtype=jnp.int32)
    source = pairs[:, 0]
    target = pairs[:, 1]
    in_moved = jnp.any(moved[:, :, None] == slot_ids[None, None, :], axis=1)
    as_source = source[:, None] == inst_ids[None, :]
    as_target = target[:, None] == inst_ids[None, :]
    leaving = jnp.any(as_source[:, :, None] & in_moved[:, None, :], axis=0)
    arriving_hit = as_target[:, :, None] & in_moved[:, None, :]
    arriving = jnp.any(arriving_hit, axis=0)
    from_pair = lax.optimization_barrier(jnp.sum(jnp.where(arriving_hit, source[:, None, None], 0), axis=0)).astype(jnp.int32)
    anchor = jnp.where(arriving, from_pair, inst_ids[:, None]).astype(jnp.int32)
    eff_len = lengths[anchor, slot_ids[None, :]]
    scale = 1.0 / math.sqrt(HD)
    pool_heads = kv_pool[:, :, ::REP]
    qall = queries.reshape(STEPS, N_INST, REQ, KVH, GQA, HD)
    fall = fresh_kv.reshape(STEPS, N_INST, REQ, KVS, 2 * HD)[:, :, :, ::REP]
    step_ok = jnp.arange(STEPS)[None, :] <= jnp.arange(STEPS)[:, None]

    def one_instance(i):
        org = anchor[i]
        tables = block_table[org[:, None], slot_ids[:, None], jnp.arange(NBLK)[None, :]]
        cache = pool_heads[org[:, None], tables]
        cache = cache.transpose(0, 2, 1, 3, 4).reshape(REQ, KVH, CTX, 2 * HD).astype(jnp.float32)
        keys = cache[..., :HD]
        vals = cache[..., HD:]
        qi = lax.dynamic_index_in_dim(qall, i, 1, False).astype(jnp.float32)
        fi = lax.dynamic_index_in_dim(fall, i, 1, False).astype(jnp.float32)
        s_cache = jnp.einsum('trgqd,rgcd->trgqc', qi, keys) * scale
        pos_ok = jnp.arange(CTX)[None, :] < eff_len[i][:, None]
        s_cache = jnp.where(pos_ok[None, :, None, None, :], s_cache, -1e+30)
        s_new = jnp.einsum('trgqd,urgd->trgqu', qi, fi[..., :HD]) * scale
        s_new = jnp.where(step_ok[:, None, None, None, :], s_new, -1e+30)
        scores = jnp.concatenate([s_cache, s_new], axis=-1)
        top = lax.optimization_barrier(jnp.max(scores, axis=-1, keepdims=True))
        expo = jnp.exp(scores - top)
        weights = (expo / lax.optimization_barrier(jnp.sum(expo, axis=-1, keepdims=True))).astype(jnp.bfloat16).astype(jnp.float32)
        out = jnp.einsum('trgqc,rgcd->trgqd', weights[..., :CTX], vals)
        out = out + jnp.einsum('trgqu,urgd->trgqd', weights[..., CTX:], fi[..., HD:])
        attention = out.astype(jnp.bfloat16).reshape(STEPS, REQ, HEADS * HD)
        attention = jnp.where(leaving[i][None, :, None], jnp.zeros_like(attention), attention)
        mixed = jnp.dot(attention.reshape(STEPS * REQ, HEADS * HD), out_weight, preferred_element_type=jnp.float32)
        return mixed.astype(jnp.bfloat16).reshape(STEPS, REQ, D)
    every = lax.map(one_instance, inst_ids)
    return every.transpose(1, 0, 2, 3).reshape(STEPS, N_INST * REQ, D)
```

```python
import functools
import math

import jax
import jax.numpy as jnp
from jax import lax
from jax.experimental import pallas as pl
from jax.experimental.pallas import tpu as pltpu
from jax.sharding import PartitionSpec as P

MESH = pl.DeviceIdType.MESH
F32 = jnp.float32
BF16 = jnp.bfloat16
LANE = 128
SUB = 8
PIECE = 512
POOL_CUTS = 8
TOGETHER = 4


def kernel(
    n_inst,
    n_tp,
    table,
    lengths,
    pairs,
    moved,
    pool,
    queries,
    fresh,
    weight,
    out,
    pool_v,
    q_v,
    f_v,
    w_v,
    q32,
    f32,
    o32,
    ask,
    reply,
    attn,
    part_send,
    part_recv,
    own,
    pool_sem,
    in_sem,
    w_sem,
    ask_send,
    ask_recv,
    reply_send,
    reply_recv,
    part_ssem,
    part_rsem,
):
    steps, slots, width = q_v.shape
    n_blocks = table.shape[1]
    groups = pool_v.shape[1]
    block = pool_v.shape[2]
    span = n_blocks * block
    per_pair = moved.shape[1]
    n_pairs = pairs.shape[0]
    hpg = width // LANE // groups
    rows = steps * slots
    pieces = own.shape[0]
    scale = 1.0 / math.sqrt(LANE)
    trow = slots * SUB
    q_rows = steps * SUB
    me = lax.axis_index("inst")
    my_tp = lax.axis_index("tp")

    def inst_peer(d):
        return lax.rem(me + d, n_inst)

    def tp_peer(d):
        return lax.rem(my_tp + d, n_tp)

    q_copy = pltpu.make_async_copy(queries, q_v, in_sem.at[0])
    f_copy = pltpu.make_async_copy(fresh, f_v, in_sem.at[1])
    q_copy.start()
    f_copy.start()
    cut = pool_v.shape[0] // POOL_CUTS
    pool_copies = [
        pltpu.make_async_copy(
            pool.at[pl.ds(i * cut, cut)], pool_v.at[pl.ds(i * cut, cut)], pool_sem.at[i]
        )
        for i in range(POOL_CUTS)
    ]
    for c in pool_copies:
        c.start()

    barrier = pltpu.get_barrier_semaphore()
    for d in range(1, n_inst):
        pl.semaphore_signal(barrier, inc=1, device_id={"inst": inst_peer(d)}, device_id_type=MESH)
    for d in range(1, n_tp):
        pl.semaphore_signal(barrier, inc=1, device_id={"tp": tp_peer(d)}, device_id_type=MESH)

    zero = jnp.int32(0)
    is_source, is_target = zero, zero
    to_inst, from_inst = zero, zero
    out_slots = [zero] * per_pair
    in_slots = [zero] * per_pair
    for p in range(n_pairs):
        src = jnp.where(pairs[p, 0] == me, 1, 0)
        dst = jnp.where(pairs[p, 1] == me, 1, 0)
        is_source += src
        is_target += dst
        to_inst += src * pairs[p, 1]
        from_inst += dst * pairs[p, 0]
        for k in range(per_pair):
            out_slots[k] += src * moved[p, k]
            in_slots[k] += dst * moved[p, k]
    to_inst = jnp.where(is_source > 0, to_inst, me)
    from_inst = jnp.where(is_target > 0, from_inst, me)

    q32[...] = jnp.zeros_like(q32)
    f32[...] = jnp.zeros_like(f32)
    q_copy.wait()
    f_copy.wait()
    qs = q_v[...].astype(F32).reshape(rows, width)
    for g in range(groups):
        for h in range(hpg):
            c0 = (g * hpg + h) * LANE
            q32[g, pl.ds(h, rows, stride=SUB), :] = qs[:, c0 : c0 + LANE]
    for u in range(steps):
        row = f_v[u].astype(F32)
        for c in range(2 * groups):
            f32[c, pl.ds(u, slots, stride=SUB), :] = row[:, c * LANE : (c + 1) * LANE]

    def q_of(g, s):
        at = pl.multiple_of(s * SUB, SUB)
        return jnp.concatenate(
            [q32[g, pl.ds(t * trow + at, SUB), :] for t in range(steps)], axis=0
        ).astype(BF16)

    mine = n_inst - 1
    base_q = per_pair * groups
    masks = [
        [jnp.full((SUB, LANE), in_slots[k], jnp.int32) == s for s in range(slots)]
        for k in range(per_pair)
    ]

    def pick(k, load):
        val = load(0)
        for s in range(1, slots):
            val = jnp.where(masks[k][s], load(s), val)
        return val

    for k in range(per_pair):
        for g in range(groups):
            ask[mine, k * groups + g] = jnp.concatenate(
                [
                    pick(k, lambda s: q32[g, pl.ds(t * trow + s * SUB, SUB), :])
                    for t in range(steps)
                ],
                axis=0,
            ).astype(BF16)
    for c in range(2 * groups):
        ask[mine, base_q + c] = jnp.concatenate(
            [pick(k, lambda s: f32[c, pl.ds(s * SUB, SUB), :]) for k in range(per_pair)], axis=0
        ).astype(BF16)

    pl.semaphore_wait(barrier, n_inst + n_tp - 2)

    asks = [
        pltpu.make_async_remote_copy(
            src_ref=ask.at[mine],
            dst_ref=ask.at[d - 1],
            send_sem=ask_send.at[d - 1],
            recv_sem=ask_recv.at[d - 1],
            device_id={"inst": inst_peer(d)},
            device_id_type=MESH,
        )
        for d in range(1, n_inst)
    ]
    for c in asks:
        c.start()

    for c in pool_copies:
        c.wait()

    order = list(range(1, n_tp)) + [0]
    w_copies = {}
    for d in order:
        for i in range(pieces):
            n = d * pieces + i
            col = pl.multiple_of(tp_peer(d) * (pieces * PIECE) + i * PIECE, PIECE)
            w_copies[d, i] = pltpu.make_async_copy(
                weight.at[:, pl.ds(col, PIECE)], w_v.at[n], w_sem.at[n]
            )
            w_copies[d, i].start()

    pos = lax.broadcasted_iota(jnp.int32, (groups * q_rows, span), 1)
    new_col = lax.broadcasted_iota(jnp.int32, (groups * q_rows, 2 * SUB), 1)
    new_step = lax.rem(
        lax.broadcasted_iota(jnp.int32, (groups * q_rows, 2 * SUB), 0), q_rows
    ) // SUB
    nt = (((1,), (1,)), ((), ()))

    def attend(q_groups, fresh_tiles, base, slot, length):
        wide = []
        for g in range(groups):
            line = [jnp.zeros((q_rows, LANE), BF16)] * groups
            line[g] = q_groups[g]
            wide.append(jnp.concatenate(line, axis=1))
        q = jnp.concatenate(wide, axis=0)
        keys, vals = [], []
        for j in range(n_blocks):
            b = table[slot, j]
            keys.append(jnp.concatenate([pool_v[b, g, :, :LANE] for g in range(groups)], axis=1))
            vals.append(jnp.concatenate([pool_v[b, g, :, LANE:] for g in range(groups)], axis=1))
        keys = jnp.concatenate(keys, axis=0)
        vals = jnp.concatenate(vals, axis=0)
        k_new = jnp.concatenate([fresh_tiles[2 * g] for g in range(groups)], axis=1)
        v_new = jnp.concatenate([fresh_tiles[2 * g + 1] for g in range(groups)], axis=1)
        s_old = lax.dot_general(q, keys, nt, preferred_element_type=F32) * scale
        s_new = lax.dot_general(q, k_new, nt, preferred_element_type=F32) * scale
        s_old = jnp.where(pos < length, s_old, -1e30)
        ok = (new_col >= base) & (new_col <= new_step + base)
        s_new = jnp.where(ok, s_new, -1e30)
        top = jnp.maximum(
            jnp.max(s_old, axis=1, keepdims=True), jnp.max(s_new, axis=1, keepdims=True)
        )
        e_old = jnp.exp(s_old - top)
        e_new = jnp.exp(s_new - top)
        total = jnp.sum(e_old, axis=1, keepdims=True) + jnp.sum(e_new, axis=1, keepdims=True)
        inv = 1.0 / total
        p_old = (e_old * inv).astype(BF16)
        p_new = (e_new * inv).astype(BF16)
        o = jnp.dot(p_old, vals, preferred_element_type=F32)
        o = o + jnp.dot(p_new, v_new, preferred_element_type=F32)
        return [
            o[g * q_rows : (g + 1) * q_rows, g * LANE : (g + 1) * LANE].astype(BF16)
            for g in range(groups)
        ]

    def own_slots(first, count):
        @pl.loop(0, count // TOGETHER)
        def _(it):
            for e in range(TOGETHER):
                s = first + it * TOGETHER + e
                pair_at = pl.multiple_of((s // 2) * (2 * SUB), 2 * SUB)
                tiles = [f32[c, pl.ds(pair_at, 2 * SUB), :].astype(BF16) for c in range(2 * groups)]
                res = attend(
                    [q_of(g, s) for g in range(groups)],
                    tiles,
                    lax.rem(s, 2) * SUB,
                    s,
                    lengths[me, s],
                )
                at = pl.multiple_of(s * SUB, SUB)
                for g in range(groups):
                    r = res[g].astype(F32)
                    for t in range(steps):
                        o32[g, pl.ds(t * trow + at, SUB), :] = r[t * SUB : (t + 1) * SUB]

    half = slots // 2
    own_slots(0, half)

    for c in asks:
        c.wait_recv()
    asker = lax.rem(me - to_inst + 2 * n_inst - 1, n_inst)
    for k in range(per_pair):
        res = attend(
            [ask[asker, k * groups + g] for g in range(groups)],
            [ask[asker, base_q + c] for c in range(2 * groups)],
            k * SUB,
            out_slots[k],
            lengths[me, out_slots[k]],
        )
        for g in range(groups):
            reply[mine, k * groups + g] = res[g]
    replies = [
        pltpu.make_async_remote_copy(
            src_ref=reply.at[mine],
            dst_ref=reply.at[d - 1],
            send_sem=reply_send.at[d - 1],
            recv_sem=reply_recv.at[d - 1],
            device_id={"inst": inst_peer(d)},
            device_id_type=MESH,
        )
        for d in range(1, n_inst)
    ]
    for c in replies:
        c.start()

    own_slots(half, slots - half)

    for c in replies:
        c.wait_recv()
    answer = lax.rem(me - from_inst + 2 * n_inst - 1, n_inst)
    for g in range(groups):
        got = [reply[answer, k * groups + g].astype(F32) for k in range(per_pair)]
        for s in range(slots):
            for t in range(steps):
                r0 = t * trow + s * SUB
                val = o32[g, r0 : r0 + SUB, :]
                for k in range(per_pair):
                    at = jnp.where(is_target > 0, in_slots[k], -1)
                    hit = jnp.full((SUB, LANE), at, jnp.int32) == s
                    val = jnp.where(hit, got[k][t * SUB : (t + 1) * SUB], val)
                for k in range(per_pair):
                    at = jnp.where(is_source > 0, out_slots[k], -1)
                    hit = jnp.full((SUB, LANE), at, jnp.int32) == s
                    val = jnp.where(hit, 0.0, val)
                o32[g, r0 : r0 + SUB, :] = val
    for g in range(groups):
        for h in range(hpg):
            c0 = (g * hpg + h) * LANE
            attn[:, c0 : c0 + LANE] = o32[g, pl.ds(h, rows, stride=SUB), :].astype(BF16)

    sends = []
    for d in order:
        for i in range(pieces):
            w_copies[d, i].wait()
            part = jnp.dot(attn[...], w_v[d * pieces + i], preferred_element_type=F32)
            if d == 0:
                own[i] = part
            else:
                part_send[d - 1, i] = part.astype(BF16)
                c = pltpu.make_async_remote_copy(
                    src_ref=part_send.at[d - 1, i],
                    dst_ref=part_recv.at[d - 1, i],
                    send_sem=part_ssem.at[d - 1, i],
                    recv_sem=part_rsem.at[d - 1, i],
                    device_id={"tp": tp_peer(d)},
                    device_id_type=MESH,
                )
                c.start()
                sends.append(c)
    for c in sends:
        c.wait_recv()
    for i in range(pieces):
        total = own[i]
        for d in range(1, n_tp):
            total = total + part_recv[d - 1, i].astype(F32)
        out[:, i * PIECE : (i + 1) * PIECE] = total.astype(BF16)
    for c in asks + replies + sends:
        c.wait_send()


def on_device(n_inst, n_tp, kv_pool, block_table, lengths, pairs, moved, queries, fresh_kv, out_weight):
    pool = kv_pool[0]
    table = block_table[0]
    slots, n_blocks = table.shape
    n_pool, groups, block, wide = pool.shape
    steps, _, width = queries.shape
    per_pair = moved.shape[1]
    rows = steps * slots
    d_model = out_weight.shape[1]
    cols = d_model // n_tp
    pieces = cols // PIECE
    tiles = per_pair * groups + 2 * groups
    vm = pltpu.VMEM
    dma = pltpu.SemaphoreType.DMA
    smem = pl.BlockSpec(memory_space=pltpu.SMEM)
    hbm = pl.BlockSpec(memory_space=pl.ANY)
    out = pl.pallas_call(
        functools.partial(kernel, n_inst, n_tp),
        out_shape=jax.ShapeDtypeStruct((rows, cols), BF16),
        in_specs=[smem] * 4 + [hbm] * 4,
        out_specs=pl.BlockSpec(memory_space=pltpu.VMEM),
        scratch_shapes=[
            vm(pool.shape, BF16),
            vm(queries.shape, BF16),
            vm(fresh_kv.shape, BF16),
            vm((n_tp * pieces, width, PIECE), BF16),
            vm((groups, rows * SUB, LANE), F32),
            vm((2 * groups, slots * SUB, LANE), F32),
            vm((groups, rows * SUB, LANE), F32),
            vm((n_inst, tiles, 2 * SUB, LANE), BF16),
            vm((n_inst, per_pair * groups, 2 * SUB, LANE), BF16),
            vm((rows, width), BF16),
            vm((n_tp - 1, pieces, rows, PIECE), BF16),
            vm((n_tp - 1, pieces, rows, PIECE), BF16),
            vm((pieces, rows, PIECE), F32),
            dma((POOL_CUTS,)),
            dma((2,)),
            dma((n_tp * pieces,)),
            dma((n_inst - 1,)),
            dma((n_inst - 1,)),
            dma((n_inst - 1,)),
            dma((n_inst - 1,)),
            dma((n_tp - 1, pieces)),
            dma((n_tp - 1, pieces)),
        ],
        compiler_params=pltpu.CompilerParams(
            collective_id=0, has_side_effects=True, vmem_limit_bytes=56 * 2**20
        ),
        cost_estimate=pl.CostEstimate(
            flops=2 * rows * width * d_model,
            bytes_accessed=2 * (width * d_model + pool.size),
            transcendentals=0,
        ),
    )(table, lengths, pairs, moved, pool, queries, fresh_kv, out_weight)
    return out.reshape(steps, slots, cols)


def solution(mesh):
    in_specs = (
        P(("grp", "inst"), None, "tp", None, None),
        P(("grp", "inst"), None, None),
        P("grp", None),
        P("grp", None),
        P("grp", None),
        P(None, ("grp", "inst"), "tp"),
        P(None, ("grp", "inst"), "tp"),
        P("tp", None),
    )
    out_specs = P(None, ("grp", "inst"), "tp")
    body = functools.partial(on_device, mesh.shape["inst"], mesh.shape["tp"])
    return jax.shard_map(body, mesh=mesh, in_specs=in_specs, out_specs=out_specs, check_vma=False)
```

```python
import functools
import math

import jax
import jax.numpy as jnp
from jax import lax
from jax.experimental import pallas as pl
from jax.experimental.pallas import tpu as pltpu
from jax.sharding import PartitionSpec as P

MESH = pl.DeviceIdType.MESH
F32 = jnp.float32
BF16 = jnp.bfloat16
LANE = 128
SUB = 8
PIECE = 512
POOL_CUTS = 8
TOGETHER = 4


def kernel(
    n_inst,
    n_tp,
    table,
    lengths,
    pairs,
    moved,
    pool,
    queries,
    fresh,
    weight,
    out,
    pool_v,
    q_v,
    f_v,
    w_v,
    q32,
    f32,
    o32,
    ask,
    reply,
    attn,
    part_send,
    part_recv,
    own,
    pool_sem,
    in_sem,
    w_sem,
    ask_send,
    ask_recv,
    reply_send,
    reply_recv,
    part_ssem,
    part_rsem,
):
    steps, slots, width = q_v.shape
    n_blocks = table.shape[1]
    groups = pool_v.shape[1]
    block = pool_v.shape[2]
    span = n_blocks * block
    per_pair = moved.shape[1]
    n_pairs = pairs.shape[0]
    hpg = width // LANE // groups
    rows = steps * slots
    pieces = own.shape[0]
    scale = 1.0 / math.sqrt(LANE)
    trow = slots * SUB
    q_rows = steps * SUB
    me = lax.axis_index("inst")
    my_tp = lax.axis_index("tp")

    def inst_peer(d):
        return lax.rem(me + d, n_inst)

    def tp_peer(d):
        return lax.rem(my_tp + d, n_tp)

    q_copy = pltpu.make_async_copy(queries, q_v, in_sem.at[0])
    f_copy = pltpu.make_async_copy(fresh, f_v, in_sem.at[1])
    q_copy.start()
    f_copy.start()
    cut = pool_v.shape[0] // POOL_CUTS
    pool_copies = [
        pltpu.make_async_copy(
            pool.at[pl.ds(i * cut, cut)], pool_v.at[pl.ds(i * cut, cut)], pool_sem.at[i]
        )
        for i in range(POOL_CUTS)
    ]
    for c in pool_copies:
        c.start()
    order = [(d, i) for i in range(pieces) for d in list(range(1, n_tp)) + [0]]
    w_copies = {}
    for d, i in order:
        n = d * pieces + i
        col = pl.multiple_of(tp_peer(d) * (pieces * PIECE) + i * PIECE, PIECE)
        w_copies[d, i] = pltpu.make_async_copy(
            weight.at[:, pl.ds(col, PIECE)], w_v.at[n], w_sem.at[n]
        )
        w_copies[d, i].start()

    barrier = pltpu.get_barrier_semaphore()
    for d in range(1, n_inst):
        pl.semaphore_signal(barrier, inc=1, device_id={"inst": inst_peer(d)}, device_id_type=MESH)
    for d in range(1, n_tp):
        pl.semaphore_signal(barrier, inc=1, device_id={"tp": tp_peer(d)}, device_id_type=MESH)

    zero = jnp.int32(0)
    is_source, is_target = zero, zero
    to_inst, from_inst = zero, zero
    out_slots = [zero] * per_pair
    in_slots = [zero] * per_pair
    for p in range(n_pairs):
        src = jnp.where(pairs[p, 0] == me, 1, 0)
        dst = jnp.where(pairs[p, 1] == me, 1, 0)
        is_source += src
        is_target += dst
        to_inst += src * pairs[p, 1]
        from_inst += dst * pairs[p, 0]
        for k in range(per_pair):
            out_slots[k] += src * moved[p, k]
            in_slots[k] += dst * moved[p, k]
    to_inst = jnp.where(is_source > 0, to_inst, me)
    from_inst = jnp.where(is_target > 0, from_inst, me)

    q32[...] = jnp.zeros_like(q32)
    f32[...] = jnp.zeros_like(f32)
    q_copy.wait()
    f_copy.wait()
    qs = q_v[...].astype(F32).reshape(rows, width)
    for g in range(groups):
        for h in range(hpg):
            c0 = (g * hpg + h) * LANE
            q32[g, pl.ds(h, rows, stride=SUB), :] = qs[:, c0 : c0 + LANE]
    for u in range(steps):
        row = f_v[u].astype(F32)
        for c in range(2 * groups):
            f32[c, pl.ds(u, slots, stride=SUB), :] = row[:, c * LANE : (c + 1) * LANE]

    def q_of(g, s):
        at = pl.multiple_of(s * SUB, SUB)
        return jnp.concatenate(
            [q32[g, pl.ds(t * trow + at, SUB), :] for t in range(steps)], axis=0
        ).astype(BF16)

    mine = n_inst - 1
    base_q = per_pair * groups
    masks = [
        [jnp.full((SUB, LANE), in_slots[k], jnp.int32) == s for s in range(slots)]
        for k in range(per_pair)
    ]

    def pick(k, load):
        val = load(0)
        for s in range(1, slots):
            val = jnp.where(masks[k][s], load(s), val)
        return val

    for k in range(per_pair):
        for g in range(groups):
            ask[mine, k * groups + g] = jnp.concatenate(
                [
                    pick(k, lambda s: q32[g, pl.ds(t * trow + s * SUB, SUB), :])
                    for t in range(steps)
                ],
                axis=0,
            ).astype(BF16)
    for c in range(2 * groups):
        ask[mine, base_q + c] = jnp.concatenate(
            [pick(k, lambda s: f32[c, pl.ds(s * SUB, SUB), :]) for k in range(per_pair)], axis=0
        ).astype(BF16)

    pl.semaphore_wait(barrier, n_inst + n_tp - 2)

    asks = [
        pltpu.make_async_remote_copy(
            src_ref=ask.at[mine],
            dst_ref=ask.at[d - 1],
            send_sem=ask_send.at[d - 1],
            recv_sem=ask_recv.at[d - 1],
            device_id={"inst": inst_peer(d)},
            device_id_type=MESH,
        )
        for d in range(1, n_inst)
    ]
    for c in asks:
        c.start()

    for c in pool_copies:
        c.wait()

    pos = lax.broadcasted_iota(jnp.int32, (groups * q_rows, span), 1)
    new_col = lax.broadcasted_iota(jnp.int32, (groups * q_rows, 2 * SUB), 1)
    new_step = lax.rem(
        lax.broadcasted_iota(jnp.int32, (groups * q_rows, 2 * SUB), 0), q_rows
    ) // SUB
    nt = (((1,), (1,)), ((), ()))

    def attend(q_groups, fresh_tiles, base, slot, length):
        wide = []
        for g in range(groups):
            line = [jnp.zeros((q_rows, LANE), BF16)] * groups
            line[g] = q_groups[g]
            wide.append(jnp.concatenate(line, axis=1))
        q = jnp.concatenate(wide, axis=0)
        keys, vals = [], []
        for j in range(n_blocks):
            b = table[slot, j]
            keys.append(jnp.concatenate([pool_v[b, g, :, :LANE] for g in range(groups)], axis=1))
            vals.append(jnp.concatenate([pool_v[b, g, :, LANE:] for g in range(groups)], axis=1))
        keys = jnp.concatenate(keys, axis=0)
        vals = jnp.concatenate(vals, axis=0)
        k_new = jnp.concatenate([fresh_tiles[2 * g] for g in range(groups)], axis=1)
        v_new = jnp.concatenate([fresh_tiles[2 * g + 1] for g in range(groups)], axis=1)
        s_old = lax.dot_general(q, keys, nt, preferred_element_type=F32) * scale
        s_new = lax.dot_general(q, k_new, nt, preferred_element_type=F32) * scale
        s_old = jnp.where(pos < length, s_old, -1e30)
        ok = (new_col >= base) & (new_col <= new_step + base)
        s_new = jnp.where(ok, s_new, -1e30)
        top = jnp.maximum(
            jnp.max(s_old, axis=1, keepdims=True), jnp.max(s_new, axis=1, keepdims=True)
        )
        e_old = jnp.exp(s_old - top)
        e_new = jnp.exp(s_new - top)
        total = jnp.sum(e_old, axis=1, keepdims=True) + jnp.sum(e_new, axis=1, keepdims=True)
        inv = 1.0 / total
        p_old = (e_old * inv).astype(BF16)
        p_new = (e_new * inv).astype(BF16)
        o = jnp.dot(p_old, vals, preferred_element_type=F32)
        o = o + jnp.dot(p_new, v_new, preferred_element_type=F32)
        return [
            o[g * q_rows : (g + 1) * q_rows, g * LANE : (g + 1) * LANE].astype(BF16)
            for g in range(groups)
        ]

    def own_slots(first, count):
        @pl.loop(0, count // TOGETHER)
        def _(it):
            for e in range(TOGETHER):
                s = first + it * TOGETHER + e
                pair_at = pl.multiple_of((s // 2) * (2 * SUB), 2 * SUB)
                tiles = [f32[c, pl.ds(pair_at, 2 * SUB), :].astype(BF16) for c in range(2 * groups)]
                res = attend(
                    [q_of(g, s) for g in range(groups)],
                    tiles,
                    lax.rem(s, 2) * SUB,
                    s,
                    lengths[me, s],
                )
                at = pl.multiple_of(s * SUB, SUB)
                for g in range(groups):
                    r = res[g].astype(F32)
                    for t in range(steps):
                        o32[g, pl.ds(t * trow + at, SUB), :] = r[t * SUB : (t + 1) * SUB]

    own_slots(0, slots)

    for c in asks:
        c.wait_recv()
    asker = lax.rem(me - to_inst + 2 * n_inst - 1, n_inst)
    away = [jnp.where(is_source > 0, out_slots[k], -1) for k in range(per_pair)]
    here = [jnp.where(is_target > 0, in_slots[k], -1) for k in range(per_pair)]
    got = [
        attend(
            [ask[asker, k * groups + g] for g in range(groups)],
            [ask[asker, base_q + c] for c in range(2 * groups)],
            k * SUB,
            out_slots[k],
            lengths[me, out_slots[k]],
        )
        for k in range(per_pair)
    ]
    for s in range(slots):
        hits = [jnp.full((SUB, LANE), away[k], jnp.int32) == s for k in range(per_pair)]
        for g in range(groups):
            for t in range(steps):
                r0 = t * trow + s * SUB
                val = o32[g, r0 : r0 + SUB, :]
                for k in range(per_pair):
                    val = jnp.where(hits[k], got[k][g][t * SUB : (t + 1) * SUB].astype(F32), val)
                o32[g, r0 : r0 + SUB, :] = val
    for g in range(groups):
        for h in range(hpg):
            c0 = (g * hpg + h) * LANE
            attn[:, c0 : c0 + LANE] = o32[g, pl.ds(h, rows, stride=SUB), :].astype(BF16)

    sends = {}
    for d, i in order:
        w_copies[d, i].wait()
        part = jnp.dot(attn[...], w_v[d * pieces + i], preferred_element_type=F32)
        if d == 0:
            own[i] = part
        else:
            part_send[d - 1, i] = part.astype(BF16)
            c = pltpu.make_async_remote_copy(
                src_ref=part_send.at[d - 1, i],
                dst_ref=part_recv.at[d - 1, i],
                send_sem=part_ssem.at[d - 1, i],
                recv_sem=part_rsem.at[d - 1, i],
                device_id={"tp": tp_peer(d)},
                device_id_type=MESH,
            )
            c.start()
            sends[d, i] = c

    n_back = reply.shape[1]
    b_row = lax.broadcasted_iota(jnp.int32, (n_back, rows), 0)
    b_col = lax.broadcasted_iota(jnp.int32, (n_back, rows), 1)
    back = jnp.zeros((n_back, PIECE), F32)
    totals = []
    for i in range(pieces):
        total = own[i]
        for d in range(1, n_tp):
            sends[d, i].wait_recv()
            total = total + part_recv[d - 1, i].astype(F32)
        total = total.astype(BF16)
        totals.append(total)
        hot = jnp.zeros((n_back, rows), F32)
        for k in range(per_pair):
            for t in range(steps):
                at = (i * per_pair + k) * steps + t
                hot = jnp.where((b_row == at) & (b_col == out_slots[k] + t * slots), 1.0, hot)
        back = back + jnp.dot(hot.astype(BF16), total, preferred_element_type=F32)
    reply[mine] = back.astype(BF16)
    replies = [
        pltpu.make_async_remote_copy(
            src_ref=reply.at[mine],
            dst_ref=reply.at[d - 1],
            send_sem=reply_send.at[d - 1],
            recv_sem=reply_recv.at[d - 1],
            device_id={"inst": inst_peer(d)},
            device_id_type=MESH,
        )
        for d in range(1, n_inst)
    ]
    for c in replies:
        c.start()
    answer = lax.rem(me - from_inst + 2 * n_inst - 1, n_inst)
    slot_of = lax.rem(lax.broadcasted_iota(jnp.int32, (rows, PIECE), 0), slots)
    gone = slot_of == away[0]
    come = slot_of == here[0]
    for k in range(1, per_pair):
        gone = gone | (slot_of == away[k])
        come = come | (slot_of == here[k])
    f_row = lax.broadcasted_iota(jnp.int32, (rows, n_back), 0)
    f_col = lax.broadcasted_iota(jnp.int32, (rows, n_back), 1)
    for c in replies:
        c.wait_recv()
    result = reply[answer]
    for i in range(pieces):
        hot = jnp.zeros((rows, n_back), F32)
        for k in range(per_pair):
            for t in range(steps):
                at = (i * per_pair + k) * steps + t
                hot = jnp.where((f_col == at) & (f_row == in_slots[k] + t * slots), 1.0, hot)
        moved_in = jnp.dot(hot.astype(BF16), result, preferred_element_type=F32)
        val = jnp.where(come, moved_in, totals[i].astype(F32))
        val = jnp.where(gone, 0.0, val)
        out[:, i * PIECE : (i + 1) * PIECE] = val.astype(BF16)
    for c in asks + replies + list(sends.values()):
        c.wait_send()


def on_device(n_inst, n_tp, kv_pool, block_table, lengths, pairs, moved, queries, fresh_kv, out_weight):
    pool = kv_pool[0]
    table = block_table[0]
    slots, n_blocks = table.shape
    n_pool, groups, block, wide = pool.shape
    steps, _, width = queries.shape
    per_pair = moved.shape[1]
    rows = steps * slots
    d_model = out_weight.shape[1]
    cols = d_model // n_tp
    pieces = cols // PIECE
    tiles = per_pair * groups + 2 * groups
    back = -(-(pieces * per_pair * steps) // 16) * 16
    vm = pltpu.VMEM
    dma = pltpu.SemaphoreType.DMA
    smem = pl.BlockSpec(memory_space=pltpu.SMEM)
    hbm = pl.BlockSpec(memory_space=pl.ANY)
    out = pl.pallas_call(
        functools.partial(kernel, n_inst, n_tp),
        out_shape=jax.ShapeDtypeStruct((rows, cols), BF16),
        in_specs=[smem] * 4 + [hbm] * 4,
        out_specs=pl.BlockSpec(memory_space=pltpu.VMEM),
        scratch_shapes=[
            vm(pool.shape, BF16),
            vm(queries.shape, BF16),
            vm(fresh_kv.shape, BF16),
            vm((n_tp * pieces, width, PIECE), BF16),
            vm((groups, rows * SUB, LANE), F32),
            vm((2 * groups, slots * SUB, LANE), F32),
            vm((groups, rows * SUB, LANE), F32),
            vm((n_inst, tiles, 2 * SUB, LANE), BF16),
            vm((n_inst, back, PIECE), BF16),
            vm((rows, width), BF16),
            vm((n_tp - 1, pieces, rows, PIECE), BF16),
            vm((n_tp - 1, pieces, rows, PIECE), BF16),
            vm((pieces, rows, PIECE), F32),
            dma((POOL_CUTS,)),
            dma((2,)),
            dma((n_tp * pieces,)),
            dma((n_inst - 1,)),
            dma((n_inst - 1,)),
            dma((n_inst - 1,)),
            dma((n_inst - 1,)),
            dma((n_tp - 1, pieces)),
            dma((n_tp - 1, pieces)),
        ],
        compiler_params=pltpu.CompilerParams(
            collective_id=0, has_side_effects=True, vmem_limit_bytes=56 * 2**20
        ),
        cost_estimate=pl.CostEstimate(
            flops=2 * rows * width * d_model,
            bytes_accessed=2 * (width * d_model + pool.size),
            transcendentals=0,
        ),
    )(table, lengths, pairs, moved, pool, queries, fresh_kv, out_weight)
    return out.reshape(steps, slots, cols)


def solution(mesh):
    in_specs = (
        P(("grp", "inst"), None, "tp", None, None),
        P(("grp", "inst"), None, None),
        P("grp", None),
        P("grp", None),
        P("grp", None),
        P(None, ("grp", "inst"), "tp"),
        P(None, ("grp", "inst"), "tp"),
        P("tp", None),
    )
    out_specs = P(None, ("grp", "inst"), "tp")
    body = functools.partial(on_device, mesh.shape["inst"], mesh.shape["tp"])
    return jax.shard_map(body, mesh=mesh, in_specs=in_specs, out_specs=out_specs, check_vma=False)
```

```python
import functools
import math

import jax
import jax.numpy as jnp
from jax import lax
from jax.experimental import pallas as pl
from jax.experimental.pallas import tpu as pltpu
from jax.sharding import PartitionSpec as P

MESH = pl.DeviceIdType.MESH
F32 = jnp.float32
BF16 = jnp.bfloat16
LANE = 128
SUB = 8
PIECE = 512
POOL_CUTS = 8
TOGETHER = 4


def kernel(
    n_inst,
    n_tp,
    table,
    lengths,
    pairs,
    moved,
    pool,
    queries,
    fresh,
    weight,
    out,
    pool_v,
    q_v,
    f_v,
    w_v,
    q32,
    f32,
    o32,
    ask,
    reply,
    attn,
    part_send,
    part_recv,
    own,
    pool_sem,
    in_sem,
    w_sem,
    ask_send,
    ask_recv,
    reply_send,
    reply_recv,
    part_ssem,
    part_rsem,
):
    steps, slots, width = q_v.shape
    n_blocks = table.shape[1]
    groups = pool_v.shape[1]
    block = pool_v.shape[2]
    span = n_blocks * block
    per_pair = moved.shape[1]
    n_pairs = pairs.shape[0]
    hpg = width // LANE // groups
    rows = steps * slots
    pieces = own.shape[0]
    scale = 1.0 / math.sqrt(LANE)
    trow = slots * SUB
    q_rows = steps * SUB
    me = lax.axis_index("inst")
    my_tp = lax.axis_index("tp")

    def inst_peer(d):
        return lax.rem(me + d, n_inst)

    def tp_peer(d):
        return lax.rem(my_tp + d, n_tp)

    q_copy = pltpu.make_async_copy(queries, q_v, in_sem.at[0])
    f_copy = pltpu.make_async_copy(fresh, f_v, in_sem.at[1])
    q_copy.start()
    f_copy.start()
    cut = pool_v.shape[0] // POOL_CUTS
    pool_copies = [
        pltpu.make_async_copy(
            pool.at[pl.ds(i * cut, cut)], pool_v.at[pl.ds(i * cut, cut)], pool_sem.at[i]
        )
        for i in range(POOL_CUTS)
    ]
    for c in pool_copies:
        c.start()

    barrier = pltpu.get_barrier_semaphore()
    for d in range(1, n_inst):
        pl.semaphore_signal(barrier, inc=1, device_id={"inst": inst_peer(d)}, device_id_type=MESH)
    for d in range(1, n_tp):
        pl.semaphore_signal(barrier, inc=1, device_id={"tp": tp_peer(d)}, device_id_type=MESH)

    zero = jnp.int32(0)
    is_source, is_target = zero, zero
    to_inst, from_inst = zero, zero
    out_slots = [zero] * per_pair
    in_slots = [zero] * per_pair
    for p in range(n_pairs):
        src = jnp.where(pairs[p, 0] == me, 1, 0)
        dst = jnp.where(pairs[p, 1] == me, 1, 0)
        is_source += src
        is_target += dst
        to_inst += src * pairs[p, 1]
        from_inst += dst * pairs[p, 0]
        for k in range(per_pair):
            out_slots[k] += src * moved[p, k]
            in_slots[k] += dst * moved[p, k]
    to_inst = jnp.where(is_source > 0, to_inst, me)
    from_inst = jnp.where(is_target > 0, from_inst, me)

    q32[...] = jnp.zeros_like(q32)
    f32[...] = jnp.zeros_like(f32)
    q_copy.wait()
    f_copy.wait()
    qs = q_v[...].astype(F32).reshape(rows, width)
    for g in range(groups):
        for h in range(hpg):
            c0 = (g * hpg + h) * LANE
            q32[g, pl.ds(h, rows, stride=SUB), :] = qs[:, c0 : c0 + LANE]
    for u in range(steps):
        row = f_v[u].astype(F32)
        for c in range(2 * groups):
            f32[c, pl.ds(u, slots, stride=SUB), :] = row[:, c * LANE : (c + 1) * LANE]

    def q_of(g, s):
        at = pl.multiple_of(s * SUB, SUB)
        return jnp.concatenate(
            [q32[g, pl.ds(t * trow + at, SUB), :] for t in range(steps)], axis=0
        ).astype(BF16)

    mine = n_inst - 1
    base_q = per_pair * groups
    masks = [
        [jnp.full((SUB, LANE), in_slots[k], jnp.int32) == s for s in range(slots)]
        for k in range(per_pair)
    ]

    def pick(k, load):
        val = load(0)
        for s in range(1, slots):
            val = jnp.where(masks[k][s], load(s), val)
        return val

    for k in range(per_pair):
        for g in range(groups):
            ask[mine, k * groups + g] = jnp.concatenate(
                [
                    pick(k, lambda s: q32[g, pl.ds(t * trow + s * SUB, SUB), :])
                    for t in range(steps)
                ],
                axis=0,
            ).astype(BF16)
    for c in range(2 * groups):
        ask[mine, base_q + c] = jnp.concatenate(
            [pick(k, lambda s: f32[c, pl.ds(s * SUB, SUB), :]) for k in range(per_pair)], axis=0
        ).astype(BF16)

    pl.semaphore_wait(barrier, n_inst + n_tp - 2)

    asks = [
        pltpu.make_async_remote_copy(
            src_ref=ask.at[mine],
            dst_ref=ask.at[d - 1],
            send_sem=ask_send.at[d - 1],
            recv_sem=ask_recv.at[d - 1],
            device_id={"inst": inst_peer(d)},
            device_id_type=MESH,
        )
        for d in range(1, n_inst)
    ]
    for c in asks:
        c.start()

    for c in pool_copies:
        c.wait()

    middle = n_tp // 2
    order = [middle] + [d for d in range(1, n_tp) if d != middle] + [0]
    w_copies = {}
    for d in order:
        for i in range(pieces):
            n = d * pieces + i
            col = pl.multiple_of(tp_peer(d) * (pieces * PIECE) + i * PIECE, PIECE)
            w_copies[d, i] = pltpu.make_async_copy(
                weight.at[:, pl.ds(col, PIECE)], w_v.at[n], w_sem.at[n]
            )
            w_copies[d, i].start()

    pos = lax.broadcasted_iota(jnp.int32, (groups * q_rows, span), 1)
    new_col = lax.broadcasted_iota(jnp.int32, (groups * q_rows, 2 * SUB), 1)
    new_step = lax.rem(
        lax.broadcasted_iota(jnp.int32, (groups * q_rows, 2 * SUB), 0), q_rows
    ) // SUB
    nt = (((1,), (1,)), ((), ()))

    def attend(q_groups, fresh_tiles, base, slot, length):
        wide = []
        for g in range(groups):
            line = [jnp.zeros((q_rows, LANE), BF16)] * groups
            line[g] = q_groups[g]
            wide.append(jnp.concatenate(line, axis=1))
        q = jnp.concatenate(wide, axis=0)
        keys, vals = [], []
        for j in range(n_blocks):
            b = table[slot, j]
            keys.append(jnp.concatenate([pool_v[b, g, :, :LANE] for g in range(groups)], axis=1))
            vals.append(jnp.concatenate([pool_v[b, g, :, LANE:] for g in range(groups)], axis=1))
        keys = jnp.concatenate(keys, axis=0)
        vals = jnp.concatenate(vals, axis=0)
        k_new = jnp.concatenate([fresh_tiles[2 * g] for g in range(groups)], axis=1)
        v_new = jnp.concatenate([fresh_tiles[2 * g + 1] for g in range(groups)], axis=1)
        s_old = lax.dot_general(q, keys, nt, preferred_element_type=F32) * scale
        s_new = lax.dot_general(q, k_new, nt, preferred_element_type=F32) * scale
        s_old = jnp.where(pos < length, s_old, -1e30)
        ok = (new_col >= base) & (new_col <= new_step + base)
        s_new = jnp.where(ok, s_new, -1e30)
        top = jnp.maximum(
            jnp.max(s_old, axis=1, keepdims=True), jnp.max(s_new, axis=1, keepdims=True)
        )
        e_old = jnp.exp(s_old - top)
        e_new = jnp.exp(s_new - top)
        total = jnp.sum(e_old, axis=1, keepdims=True) + jnp.sum(e_new, axis=1, keepdims=True)
        inv = 1.0 / total
        p_old = (e_old * inv).astype(BF16)
        p_new = (e_new * inv).astype(BF16)
        o = jnp.dot(p_old, vals, preferred_element_type=F32)
        o = o + jnp.dot(p_new, v_new, preferred_element_type=F32)
        return [
            o[g * q_rows : (g + 1) * q_rows, g * LANE : (g + 1) * LANE].astype(BF16)
            for g in range(groups)
        ]

    def own_slots(first, count):
        @pl.loop(0, count // TOGETHER)
        def _(it):
            for e in range(TOGETHER):
                s = first + it * TOGETHER + e
                pair_at = pl.multiple_of((s // 2) * (2 * SUB), 2 * SUB)
                tiles = [f32[c, pl.ds(pair_at, 2 * SUB), :].astype(BF16) for c in range(2 * groups)]
                res = attend(
                    [q_of(g, s) for g in range(groups)],
                    tiles,
                    lax.rem(s, 2) * SUB,
                    s,
                    lengths[me, s],
                )
                at = pl.multiple_of(s * SUB, SUB)
                for g in range(groups):
                    r = res[g].astype(F32)
                    for t in range(steps):
                        o32[g, pl.ds(t * trow + at, SUB), :] = r[t * SUB : (t + 1) * SUB]

    half = slots // 2
    own_slots(0, half)

    for c in asks:
        c.wait_recv()
    asker = lax.rem(me - to_inst + 2 * n_inst - 1, n_inst)
    for k in range(per_pair):
        res = attend(
            [ask[asker, k * groups + g] for g in range(groups)],
            [ask[asker, base_q + c] for c in range(2 * groups)],
            k * SUB,
            out_slots[k],
            lengths[me, out_slots[k]],
        )
        for g in range(groups):
            reply[mine, k * groups + g] = res[g]
    replies = [
        pltpu.make_async_remote_copy(
            src_ref=reply.at[mine],
            dst_ref=reply.at[d - 1],
            send_sem=reply_send.at[d - 1],
            recv_sem=reply_recv.at[d - 1],
            device_id={"inst": inst_peer(d)},
            device_id_type=MESH,
        )
        for d in range(1, n_inst)
    ]
    for c in replies:
        c.start()

    own_slots(half, slots - half)

    for c in replies:
        c.wait_recv()
    answer = lax.rem(me - from_inst + 2 * n_inst - 1, n_inst)
    for g in range(groups):
        got = [reply[answer, k * groups + g].astype(F32) for k in range(per_pair)]
        for s in range(slots):
            for t in range(steps):
                r0 = t * trow + s * SUB
                val = o32[g, r0 : r0 + SUB, :]
                for k in range(per_pair):
                    at = jnp.where(is_target > 0, in_slots[k], -1)
                    hit = jnp.full((SUB, LANE), at, jnp.int32) == s
                    val = jnp.where(hit, got[k][t * SUB : (t + 1) * SUB], val)
                for k in range(per_pair):
                    at = jnp.where(is_source > 0, out_slots[k], -1)
                    hit = jnp.full((SUB, LANE), at, jnp.int32) == s
                    val = jnp.where(hit, 0.0, val)
                o32[g, r0 : r0 + SUB, :] = val
    for g in range(groups):
        for h in range(hpg):
            c0 = (g * hpg + h) * LANE
            attn[:, c0 : c0 + LANE] = o32[g, pl.ds(h, rows, stride=SUB), :].astype(BF16)

    sends = []
    for d in order:
        for i in range(pieces):
            w_copies[d, i].wait()
            part = jnp.dot(attn[...], w_v[d * pieces + i], preferred_element_type=F32)
            if d == 0:
                own[i] = part
            else:
                part_send[d - 1, i] = part.astype(BF16)
                c = pltpu.make_async_remote_copy(
                    src_ref=part_send.at[d - 1, i],
                    dst_ref=part_recv.at[d - 1, i],
                    send_sem=part_ssem.at[d - 1, i],
                    recv_sem=part_rsem.at[d - 1, i],
                    device_id={"tp": tp_peer(d)},
                    device_id_type=MESH,
                )
                c.start()
                sends.append(c)
    for c in sends:
        c.wait_recv()
    for i in range(pieces):
        total = own[i]
        for d in range(1, n_tp):
            total = total + part_recv[d - 1, i].astype(F32)
        out[:, i * PIECE : (i + 1) * PIECE] = total.astype(BF16)
    for c in asks + replies + sends:
        c.wait_send()


def on_device(n_inst, n_tp, kv_pool, block_table, lengths, pairs, moved, queries, fresh_kv, out_weight):
    pool = kv_pool[0]
    table = block_table[0]
    slots, n_blocks = table.shape
    n_pool, groups, block, wide = pool.shape
    steps, _, width = queries.shape
    per_pair = moved.shape[1]
    rows = steps * slots
    d_model = out_weight.shape[1]
    cols = d_model // n_tp
    pieces = cols // PIECE
    tiles = per_pair * groups + 2 * groups
    vm = pltpu.VMEM
    dma = pltpu.SemaphoreType.DMA
    smem = pl.BlockSpec(memory_space=pltpu.SMEM)
    hbm = pl.BlockSpec(memory_space=pl.ANY)
    out = pl.pallas_call(
        functools.partial(kernel, n_inst, n_tp),
        out_shape=jax.ShapeDtypeStruct((rows, cols), BF16),
        in_specs=[smem] * 4 + [hbm] * 4,
        out_specs=pl.BlockSpec(memory_space=pltpu.VMEM),
        scratch_shapes=[
            vm(pool.shape, BF16),
            vm(queries.shape, BF16),
            vm(fresh_kv.shape, BF16),
            vm((n_tp * pieces, width, PIECE), BF16),
            vm((groups, rows * SUB, LANE), F32),
            vm((2 * groups, slots * SUB, LANE), F32),
            vm((groups, rows * SUB, LANE), F32),
            vm((n_inst, tiles, 2 * SUB, LANE), BF16),
            vm((n_inst, per_pair * groups, 2 * SUB, LANE), BF16),
            vm((rows, width), BF16),
            vm((n_tp - 1, pieces, rows, PIECE), BF16),
            vm((n_tp - 1, pieces, rows, PIECE), BF16),
            vm((pieces, rows, PIECE), F32),
            dma((POOL_CUTS,)),
            dma((2,)),
            dma((n_tp * pieces,)),
            dma((n_inst - 1,)),
            dma((n_inst - 1,)),
            dma((n_inst - 1,)),
            dma((n_inst - 1,)),
            dma((n_tp - 1, pieces)),
            dma((n_tp - 1, pieces)),
        ],
        compiler_params=pltpu.CompilerParams(
            collective_id=0, has_side_effects=True, vmem_limit_bytes=56 * 2**20
        ),
        cost_estimate=pl.CostEstimate(
            flops=2 * rows * width * d_model,
            bytes_accessed=2 * (width * d_model + pool.size),
            transcendentals=0,
        ),
    )(table, lengths, pairs, moved, pool, queries, fresh_kv, out_weight)
    return out.reshape(steps, slots, cols)


def solution(mesh):
    in_specs = (
        P(("grp", "inst"), None, "tp", None, None),
        P(("grp", "inst"), None, None),
        P("grp", None),
        P("grp", None),
        P("grp", None),
        P(None, ("grp", "inst"), "tp"),
        P(None, ("grp", "inst"), "tp"),
        P("tp", None),
    )
    out_specs = P(None, ("grp", "inst"), "tp")
    body = functools.partial(on_device, mesh.shape["inst"], mesh.shape["tp"])
    return jax.shard_map(body, mesh=mesh, in_specs=in_specs, out_specs=out_specs, check_vma=False)
```
